512 devices in a mesh: task: 8 (over y_lo, core), fsdp: 64 (over x, y_hi, z).
Axes of the slice: x: 4, y: 8 (y_hi: 2, y_lo: 4; y = y_hi * 4 + y_lo), z: 8, core: 2. Of those that a mesh axis runs over, the one named last changes fastest.
Arguments:
- embeddings: bfloat16 [1024, 4096], P(('task', 'fsdp')), may hold values from -6 to 6
- head_in: bfloat16 [8, 4096, 8192], P('task', None, 'fsdp'), may hold values from -0.09375 to 0.09375
- bias_in: float32 [8, 8192], P('task', 'fsdp'), may hold values from -3 to 3
- head_out: bfloat16 [8, 8192, 128], P('task', 'fsdp'), may hold values from -0.1875 to 0.1875
- bias_out: float32 [8192], P('task'), may hold values from -3 to 3
- block_owner: int32 [8, 8], P('task'), may hold values from 0 to 7, each once within a row
- targets: bfloat16 [1024, 8192], P('fsdp', 'task'), may hold values from -5 to 5
- entry_mask: int32 [1024, 8192], P('fsdp', 'task'), may hold values 0 or 1
- block_mask: int32 [128, 64], P('fsdp', 'task'), may hold values from 0 to 1
Outputs:
- head_in_grad: float32 [8, 4096, 8192], P('task', None, 'fsdp')
- bias_in_grad: float32 [8, 8192], P('task', 'fsdp')
- head_out_grad: float32 [8, 8192, 128], P('task', 'fsdp')
The draws below stay inside these ranges and needn't reach their ends.
Inputs may be any that keep to these rules, and one draw needn't show every extreme that they name: `block_owner`: each row lists every one of the 8 assay blocks of its group once.
All inputs are finite; a program needn't handle non-finite values. No bound on the sum of `entry_mask` on one device may be relied on, other than what follows from the above.
Results may differ from the reference program's by a relative error of at most 0.0043.
Values may be sent and summed in bfloat16 or wider, within the bound.
No kernel may reach another device: no remote copies, remote signals or barrier semaphores. Data moves between devices by JAX's collectives and lax.ppermute only.
A program may use at most 64 MiB of HBM per device.

```python
import math
import jax
import jax.numpy as jnp
from jax import lax

D = 4096
H = 1024
A = 128
CBLK = 8
BLOCKS = 8
COMPOUNDS = 1024
ASSAYS = 8192
N_TASK = 8


def draw_block_mask(key, part):
    key = jax.random.fold_in(key, 11)
    level_key, entry_key = jax.random.split(key)
    levels = jax.random.randint(level_key, (COMPOUNDS // CBLK, 1), 1, 9)
    entries = jax.random.randint(entry_key, (COMPOUNDS // CBLK, N_TASK * BLOCKS), 0, 8)
    return (entries < levels).astype(jnp.int32)


def with_ends(result, stream_key, least, top_value):
    longest = result.shape.index(max(result.shape))
    spots = []
    for shift in (0, 1):
        where = [jax.random.randint(jax.random.fold_in(stream_key, axis), (), 0, length) for axis, length in enumerate(result.shape)]
        where[longest] = (where[longest] + shift) % result.shape[longest]
        spots.append(tuple(where))
    return result.at[spots[0]].set(least).at[spots[1]].set(top_value)


def block_levels(rng, extent, cuts, least, largest):
    def one(dim, shards_of):
        heights = jax.random.uniform(jax.random.fold_in(jax.random.fold_in(rng, 6), dim), (shards_of,), jnp.float32, least / len(cuts), largest / len(cuts))
        return jnp.repeat(jnp.exp(heights), extent[dim] // shards_of).reshape((-1,) + (1,) * (len(extent) - dim - 1))

    factor_of = one(*cuts[0])
    for cut in cuts[1:]:
        factor_of = factor_of * one(*cut)
    return factor_of


def gaussian(key, shape, deviation, most, cuts=(), held_as=jnp.bfloat16):
    level = block_levels(key, shape, cuts, -0.22, 0.18) if cuts else 1.0
    values = jax.random.normal(key, shape, jnp.float32) * deviation * level
    return jnp.minimum(jnp.maximum(values, -most), most).astype(held_as)


def setup_inputs(seed: int = 0) -> dict:
    keys = jax.random.split(jax.random.key(seed), 10)
    return {
        "embeddings": gaussian(keys[0], (COMPOUNDS, D), 1.0, 6.0, ((0, 512),)),
        "head_in": gaussian(keys[1], (N_TASK, D, BLOCKS * H), D ** -0.5, 0.09375, ((0, 8), (2, 64))),
        "bias_in": gaussian(keys[2], (N_TASK, BLOCKS * H), 0.5, 3.0, ((0, 8), (1, 64)), jnp.float32),
        "head_out": gaussian(keys[3], (N_TASK, BLOCKS * H, A), H ** -0.5, 0.1875, ((0, 8), (1, 64))),
        "bias_out": gaussian(keys[4], (ASSAYS,), 0.5, 3.0, ((0, 8),), jnp.float32),
        "block_owner": jax.vmap(lambda own: jax.random.permutation(own, BLOCKS))(jax.random.split(keys[5], N_TASK)).reshape((N_TASK, BLOCKS)).astype(jnp.int32),
        "targets": gaussian(keys[6], (COMPOUNDS, ASSAYS), 1.0, 5.0, ((0, 64), (1, 8))),
        "entry_mask": with_ends((jax.random.randint(keys[7], (COMPOUNDS, ASSAYS), 0, 2) < 1).astype(jnp.int32), jax.random.fold_in(keys[7], 1), 0, 1),
        "block_mask": draw_block_mask(jax.random.fold_in(keys[9], 71), 0),
    }


inv_root_two = 0.7071067811865476
inv_root_two_pi = 0.3989422804014327

def gelu_parts(values):
    normal_cdf = 0.5 * (1.0 + jax.scipy.special.erf(values * inv_root_two))
    density = jnp.exp(-0.5 * values * values) * inv_root_two_pi
    return (values * normal_cdf, normal_cdf + values * density)

def reference(embeddings, head_in, bias_in, head_out, bias_out, block_owner, targets, entry_mask, block_mask):
    scaling = 1.0 / math.sqrt(COMPOUNDS)
    group_targets = targets.reshape(COMPOUNDS, N_TASK, BLOCKS * A).transpose(1, 0, 2)
    group_entries = entry_mask.reshape(COMPOUNDS, N_TASK, BLOCKS * A).transpose(1, 0, 2)
    group_blocks = block_mask.reshape(COMPOUNDS // CBLK, N_TASK, BLOCKS).transpose(1, 0, 2)
    group_bias = bias_out.reshape(N_TASK, BLOCKS, A)

    def one_group(group_items):
        weight_in, shift_in, weight_out, owners, target_rows, entry_rows, block_rows, shift_out = group_items
        pre_gelu = jnp.dot(embeddings, weight_in, preferred_element_type=jnp.float32) + shift_in
        activated, slopes = gelu_parts(pre_gelu)
        hidden = activated.astype(jnp.bfloat16)
        hidden_three = hidden.reshape(COMPOUNDS, BLOCKS, H).astype(jnp.float32)
        out_three = weight_out.reshape(BLOCKS, H, A).astype(jnp.float32)
        slot_logits = jnp.einsum('cbh,bha->cba', hidden_three, out_three)
        selector = (owners[:, None] == jnp.arange(BLOCKS, dtype=jnp.int32)[None, :]).astype(jnp.float32)
        logits = jnp.einsum('cba,bo->coa', slot_logits, selector, precision=lax.Precision.HIGHEST) + shift_out[None]
        measured = entry_rows.reshape(COMPOUNDS, BLOCKS, A) * jnp.repeat(block_rows, CBLK, axis=0)[:, :, None]
        target_three = target_rows.reshape(COMPOUNDS, BLOCKS, A).astype(jnp.float32)
        residual = (measured.astype(jnp.float32) * (logits - target_three) * scaling).astype(jnp.bfloat16)
        slot_residual = jnp.einsum('coa,bo->cba', residual.astype(jnp.float32), selector, precision=lax.Precision.HIGHEST)
        hidden_grad = jnp.einsum('cba,bha->cbh', slot_residual, out_three) * slopes.reshape(COMPOUNDS, BLOCKS, H)
        hidden_grad = hidden_grad.astype(jnp.bfloat16).reshape(COMPOUNDS, BLOCKS * H)
        grad_in = lax.dot_general(embeddings, hidden_grad, (((0,), (0,)), ((), ())), preferred_element_type=jnp.float32)
        grad_bias = lax.optimization_barrier(jnp.sum(hidden_grad.astype(jnp.float32), axis=0))
        grad_out = jnp.einsum('cbh,cba->bha', hidden_three, slot_residual).reshape(BLOCKS * H, A)
        return (grad_in, grad_bias, grad_out)
    head_in_grad, bias_in_grad, head_out_grad = lax.map(one_group, (head_in, bias_in, head_out, block_owner, group_targets, group_entries, group_blocks, group_bias))
    return (head_in_grad, bias_in_grad, head_out_grad)
```

```python
import math

import jax
import jax.numpy as jnp
from jax import lax
from jax.sharding import PartitionSpec as P

H = 1024
A = 128
CBLK = 8
ALL = ("task", "fsdp")

inv_root_two = 0.7071067811865476
inv_root_two_pi = 0.3989422804014327


def gelu_parts(values):
    normal_cdf = 0.5 * (1.0 + jax.scipy.special.erf(values * inv_root_two))
    density = jnp.exp(-0.5 * values * values) * inv_root_two_pi
    return (values * normal_cdf, normal_cdf + values * density)


def place(i):
    t, f = divmod(i, 64)
    ylo, core = divmod(t, 2)
    x, rest = divmod(f, 16)
    yhi, z = divmod(rest, 8)
    return x, yhi * 4 + ylo, z, core


def grouped(key, order):
    groups = {}
    for i in range(512):
        groups.setdefault(key(i), []).append(i)
    return [sorted(groups[k], key=order) for k in sorted(groups)]


def parity(i):
    x, y, z, core = place(i)
    return x % 2, y % 2, z % 2


def cube(i):
    x, y, z, core = place(i)
    return (x + core) % 4 // 2, (y + core) % 8 // 2, (z + core) % 8 // 2, core


CLASSES = grouped(lambda i: parity(i) + (place(i)[3],), place)
CUBES = grouped(cube, parity)
ALONG_Z = [[8 * j + z for z in range(8)] for j in range(8)]
ACROSS_Z = [[8 * j + z for j in range(8)] for z in range(8)]


def exchange(blocks, axis, groups):
    return lax.all_to_all(blocks, axis, 0, 0, tiled=True, axis_index_groups=groups)


def spread(block, axis, groups):
    copies = jnp.broadcast_to(block[None], (len(groups[0]),) + block.shape)
    return exchange(copies, axis, groups)


def local(
    embeddings, head_in, bias_in, head_out, bias_out, block_owner, targets, entry_mask, block_mask
):
    core = lax.axis_index("task") % 2
    slot = lax.axis_index("fsdp") // 8
    scaling = 1.0 / math.sqrt(1024)
    bf16, f32 = jnp.bfloat16, jnp.float32

    measured = entry_mask.reshape(16, 8, A) * jnp.repeat(block_mask, CBLK, axis=0)[:, :, None]
    pair = jnp.stack([targets.reshape(16, 8, A), measured.astype(bf16)])
    pair = pair.reshape(2, 2, 2, 2, 2, 8, A).transpose(5, 0, 3, 1, 2, 4, 6).reshape(8, 2 * 16 * A)
    selector = (block_owner[0][:, None] == jnp.arange(8, dtype=jnp.int32)[None, :]).astype(bf16)
    pair = jnp.dot(selector, pair, preferred_element_type=f32).astype(bf16).reshape(8, 32, A)
    bias_slot = lax.dynamic_slice_in_dim(
        bias_out.reshape(8, A), lax.dynamic_index_in_dim(block_owner[0], slot, keepdims=False), 1
    )

    rows = spread(embeddings, ALL, CLASSES).reshape(64, -1)
    own = spread(rows, ALL, CUBES).reshape(512, -1)
    own, pair = lax.optimization_barrier((own, pair))
    other = lax.ppermute(own, "task", [(i, i ^ 1) for i in range(8)])
    pair = exchange(pair, "fsdp", ACROSS_Z).reshape(8, 2, 16, A)

    def forward(part):
        pre = jnp.dot(part, head_in[0], preferred_element_type=f32) + bias_in[0][None, :]
        activated, slopes = gelu_parts(pre)
        hidden = activated.astype(bf16)
        return hidden, slopes, jnp.dot(hidden, head_out[0], preferred_element_type=f32)

    hidden_own, slopes_own, share_own = forward(own)
    hidden_other, slopes_other, share_other = forward(other)
    first = jnp.where(core == 0, share_own, share_other)
    second = jnp.where(core == 0, share_other, share_own)
    shares = jnp.stack([first, second]).reshape(2, 2, 2, 2, 2, 2, 2, 8, A)
    shares = shares.transpose(4, 1, 5, 6, 2, 0, 3, 7, 8).reshape(8, 128, A)
    logits = jnp.sum(exchange(shares, "fsdp", ALONG_Z).reshape(8, 128, A), axis=0) + bias_slot
    residual = pair[:, 1].reshape(128, A).astype(f32) * (
        logits - pair[:, 0].reshape(128, A).astype(f32)
    )
    residual = (residual * scaling).astype(bf16)
    back = spread(residual, "fsdp", ALONG_Z).reshape(2, 2, 2, 2, 2, 2, 2, 8, A)
    back = back.transpose(5, 1, 4, 6, 0, 2, 3, 7, 8).reshape(2, 512, A)
    res_own = jnp.where(core == 0, back[0], back[1])
    res_other = jnp.where(core == 0, back[1], back[0])

    def backward(part, hidden, slopes, res):
        grad = lax.dot_general(
            res, head_out[0], (((1,), (1,)), ((), ())), preferred_element_type=f32
        )
        grad = (grad * slopes).astype(bf16)
        rows_first = (((0,), (0,)), ((), ()))
        return (
            lax.dot_general(part, grad, rows_first, preferred_element_type=f32),
            jnp.sum(grad.astype(f32), axis=0),
            lax.dot_general(hidden, res, rows_first, preferred_element_type=f32),
        )

    one = backward(own, hidden_own, slopes_own, res_own)
    two = backward(other, hidden_other, slopes_other, res_other)
    return tuple((a + b)[None] for a, b in zip(one, two))


def solution(mesh):
    in_specs = (
        P(("task", "fsdp"), None),
        P("task", None, "fsdp"),
        P("task", "fsdp"),
        P("task", "fsdp", None),
        P("task"),
        P("task", None),
        P("fsdp", "task"),
        P("fsdp", "task"),
        P("fsdp", "task"),
    )
    out_specs = (P("task", None, "fsdp"), P("task", "fsdp"), P("task", "fsdp", None))
    return jax.shard_map(local, mesh=mesh, in_specs=in_specs, out_specs=out_specs, check_vma=False)
```

```python
import math

import jax
import jax.numpy as jnp
from jax import lax
from jax.experimental import pallas as pl
from jax.experimental.pallas import tpu as pltpu
from jax.sharding import PartitionSpec as P

H = 1024
A = 128
CBLK = 8
ALL = ("task", "fsdp")

inv_root_two = 0.7071067811865476
inv_root_two_pi = 0.3989422804014327


def gelu_parts(values):
    normal_cdf = 0.5 * (1.0 + jax.scipy.special.erf(values * inv_root_two))
    density = jnp.exp(-0.5 * values * values) * inv_root_two_pi
    return (values * normal_cdf, normal_cdf + values * density)


def place(i):
    t, f = divmod(i, 64)
    ylo, core = divmod(t, 2)
    x, rest = divmod(f, 16)
    yhi, z = divmod(rest, 8)
    return x, yhi * 4 + ylo, z, core


def flat(x, y, z, core):
    x, y, z = x % 4, y % 8, z % 8
    return (y % 4 * 2 + core) * 64 + x * 16 + y // 4 * 8 + z


def classes():
    groups = {}
    for i in range(512):
        x, y, z, core = place(i)
        groups.setdefault(((2 * x + y + 3 * z) % 8, core), []).append(i)
    return [sorted(groups[k], key=place) for k in sorted(groups)]


def from_chip(dx, dy, dz):
    pairs = []
    for i in range(512):
        x, y, z, core = place(i)
        s = 1 - 2 * core
        pairs.append((flat(x + s * dx, y + s * dy, z + s * dz, core), i))
    return pairs


CLASSES = classes()
CORES = [(i, i ^ 64) for i in range(512)]
HELD = [(0, 0), (0, 1), (2, 0), (2, 1), (1, 0), (1, 1), (3, 0), (3, 1), (4, 0)]
HELD += [(-2, 1), (-2, 0), (-1, 1), (-1, 0), (-3, 1), (-3, 0), (4, 1)]
DIRECT = 9
ALONG_Z = [[8 * j + z for z in range(8)] for j in range(8)]
ACROSS_Z = [[8 * j + z for j in range(8)] for z in range(8)]


def exchange(blocks, axis, groups):
    return lax.all_to_all(blocks, axis, 0, 0, tiled=True, axis_index_groups=groups)


def spread(block, axis, groups):
    copies = jnp.broadcast_to(block[None], (len(groups[0]),) + block.shape)
    return exchange(copies, axis, groups)


def send(block, pairs):
    return lax.ppermute(block, ALL, pairs)


def shares_kernel(spots, direct, swapped, head_out, out):
    for part, start in ((direct, 0), (swapped, DIRECT)):
        share = jnp.dot(part[...], head_out[...], preferred_element_type=jnp.float32)
        for j in range(part.shape[0] // 64):
            out[:, spots[start + j]] = share[64 * j : 64 * j + 64].reshape(8, 8, A)


def backward_kernel(
    spots, back, hidden_d, hidden_s, slopes_d, slopes_s, head_out, grad_d, grad_s, bias, out, wide, rows
):
    for z in range(8):
        wide[z] = back[z].astype(jnp.float32).reshape(16, 8, A)
    for j in range(16):
        rows[64 * j : 64 * j + 64] = wide[:, spots[j]].reshape(64, A)
    bias_sum = jnp.zeros((1, A), jnp.float32)
    out_sum = jnp.zeros((A, A), jnp.float32)
    start = 0
    for hidden, slopes, grad in ((hidden_d, slopes_d, grad_d), (hidden_s, slopes_s, grad_s)):
        count = hidden.shape[0]
        res = rows[start : start + count].astype(jnp.bfloat16)
        start += count
        held = lax.dot_general(
            res, head_out[...], (((1,), (1,)), ((), ())), preferred_element_type=jnp.float32
        )
        rounded = (held * slopes[...]).astype(jnp.bfloat16)
        grad[...] = rounded
        bias_sum += jnp.sum(rounded.astype(jnp.float32), axis=0, keepdims=True)
        out_sum += lax.dot_general(
            hidden[...], res, (((0,), (0,)), ((), ())), preferred_element_type=jnp.float32
        )
    bias[...] = bias_sum
    out[...] = out_sum


def call(kernel, outs, operands, scratch=()):
    vmem = pl.BlockSpec(memory_space=pltpu.VMEM)
    return pl.pallas_call(
        kernel,
        out_shape=[jax.ShapeDtypeStruct(shape, dtype) for shape, dtype in outs],
        in_specs=[pl.BlockSpec(memory_space=pltpu.SMEM)] + [vmem] * (len(operands) - 1),
        out_specs=[vmem] * len(outs),
        scratch_shapes=list(scratch),
        compiler_params=pltpu.CompilerParams(vmem_limit_bytes=32 * 1024 * 1024),
    )(*operands)


def local(
    embeddings, head_in, bias_in, head_out, bias_out, block_owner, targets, entry_mask, block_mask
):
    task, fsdp = lax.axis_index("task"), lax.axis_index("fsdp")
    core, ylo = task % 2, task // 2
    x, yhi, z = fsdp // 16, fsdp // 8 % 2, fsdp % 8
    slot = fsdp // 8
    scaling = 1.0 / math.sqrt(1024)
    bf16, f32, i32 = jnp.bfloat16, jnp.float32, jnp.int32

    offset = jnp.array([d for d, _ in HELD], i32) * (1 - 2 * core)
    whose = jnp.array([w for _, w in HELD], i32)
    spots = (2 * x + yhi * 4 + ylo + 3 * z + offset + 16) % 8 * 2 + (whose + core) % 2

    measured = entry_mask.reshape(16, 8, A) * jnp.repeat(block_mask, CBLK, axis=0)[:, :, None]
    pair = jnp.stack([targets.reshape(16, 8, A), measured.astype(bf16)])
    pair = pair.transpose(2, 0, 1, 3).reshape(8, 2 * 16 * A)
    selector = (block_owner[0][:, None] == jnp.arange(8, dtype=i32)[None, :]).astype(bf16)
    pair = jnp.dot(selector, pair, preferred_element_type=f32).astype(bf16).reshape(8, 32, A)
    bias_slot = lax.dynamic_slice_in_dim(
        bias_out.reshape(8, A), lax.dynamic_index_in_dim(block_owner[0], slot, keepdims=False), 1
    )

    mine = spread(embeddings, ALL, CLASSES).reshape(64, -1)
    mine, pair = lax.optimization_barrier((mine, pair))
    both = jnp.concatenate([mine, send(mine, CORES)])
    fourth = send(mine, from_chip(0, 1, 1))
    fetched = [send(both, from_chip(*d)) for d in ((1, 0, 0), (0, 1, 0), (0, 0, 1))]
    fetched = jnp.concatenate(fetched + [fourth])
    swapped = send(fetched, CORES)
    pair = exchange(pair, "fsdp", ACROSS_Z).reshape(8, 2, 16, A)

    r, q = jnp.arange(128, dtype=i32)[:, None], jnp.arange(128, dtype=i32)[None, :]
    row_z = (3 * (r // 16 + 32 - 2 * (z // 2) - z % 2 * 4 - r // 2 % 4)) % 8
    order = (q == r // 2 % 4 * 32 + r // 8 % 2 * 16 + row_z * 2 + r % 2).astype(bf16)
    target = jnp.dot(order, pair[:, 0].reshape(128, A), preferred_element_type=f32)
    measured = jnp.dot(order, pair[:, 1].reshape(128, A), preferred_element_type=f32)

    def forward(*parts):
        pre = [jnp.dot(part, head_in[0], preferred_element_type=f32) for part in parts]
        pre = jnp.concatenate(pre) + bias_in[0][None, :]
        activated, slopes = gelu_parts(pre)
        return activated.astype(bf16), slopes

    direct = jnp.concatenate([both, fetched])
    hidden_d, slopes_d = forward(direct)
    hidden_s, slopes_s = forward(swapped)
    weights = head_out[0]
    (shares,) = call(
        shares_kernel, [((8, 16, 8, A), f32)], (spots, hidden_d, hidden_s, weights)
    )
    sums = exchange(shares.reshape(8, 128, A), "fsdp", ALONG_Z).reshape(8, 128, A)
    logits = jnp.sum(sums, axis=0) + bias_slot
    residual = (measured * (logits - target) * scaling).astype(bf16)
    back = spread(residual, "fsdp", ALONG_Z).reshape(8, 128, A)
    grad_d, grad_s, bias_in_grad, head_out_grad = call(
        backward_kernel,
        [(hidden_d.shape, bf16), (hidden_s.shape, bf16), ((1, A), f32), ((A, A), f32)],
        (spots, back, hidden_d, hidden_s, slopes_d, slopes_s, weights),
        [pltpu.VMEM((8, 16, 8, A), f32), pltpu.VMEM((1024, A), f32)],
    )

    def rows_first(left, right):
        return lax.dot_general(left, right, (((0,), (0,)), ((), ())), preferred_element_type=f32)

    head_in_grad = rows_first(direct, grad_d) + rows_first(swapped, grad_s)
    return head_in_grad[None], bias_in_grad, head_out_grad[None]


def solution(mesh):
    in_specs = (
        P(("task", "fsdp"), None),
        P("task", None, "fsdp"),
        P("task", "fsdp"),
        P("task", "fsdp", None),
        P("task"),
        P("task", None),
        P("fsdp", "task"),
        P("fsdp", "task"),
        P("fsdp", "task"),
    )
    out_specs = (P("task", None, "fsdp"), P("task", "fsdp"), P("task", "fsdp", None))
    return jax.shard_map(local, mesh=mesh, in_specs=in_specs, out_specs=out_specs, check_vma=False)
```

```python
import math

import jax
import jax.numpy as jnp
from jax import lax
from jax.experimental import pallas as pl
from jax.experimental.pallas import tpu as pltpu
from jax.sharding import PartitionSpec as P

H = 1024
A = 128
CBLK = 8
ALL = ("task", "fsdp")

inv_root_two = 0.7071067811865476
inv_root_two_pi = 0.3989422804014327


def gelu_parts(values):
    normal_cdf = 0.5 * (1.0 + lax.erf(values * inv_root_two))
    density = jnp.exp(-0.5 * values * values) * inv_root_two_pi
    return (values * normal_cdf, normal_cdf + values * density)


def place(i):
    t, f = divmod(i, 64)
    ylo, core = divmod(t, 2)
    x, rest = divmod(f, 16)
    yhi, z = divmod(rest, 8)
    return x, yhi * 4 + ylo, z, core


def flat(x, y, z, core):
    x, y, z = x % 4, y % 8, z % 8
    return (y % 4 * 2 + core) * 64 + x * 16 + y // 4 * 8 + z


def classes():
    groups = {}
    for i in range(512):
        x, y, z, core = place(i)
        groups.setdefault(((2 * x + y + 3 * z) % 8, core), []).append(i)
    return [sorted(groups[k], key=place) for k in sorted(groups)]


def from_chip(dx, dy, dz):
    pairs = []
    for i in range(512):
        x, y, z, core = place(i)
        s = 1 - 2 * core
        pairs.append((flat(x + s * dx, y + s * dy, z + s * dz, core), i))
    return pairs


CLASSES = classes()
CORES = [(i, i ^ 64) for i in range(512)]
HELD = [(0, 0), (0, 1), (2, 0), (2, 1), (1, 0), (1, 1), (3, 0), (3, 1)]
HELD += [(-2, 1), (-2, 0), (-1, 1), (-1, 0), (-3, 1), (-3, 0), (4, 0), (4, 1)]
ALONG_Z = [[8 * j + z for z in range(8)] for j in range(8)]
ACROSS_Z = [[8 * j + z for j in range(8)] for z in range(8)]


def exchange(blocks, axis, groups):
    return lax.all_to_all(blocks, axis, 0, 0, tiled=True, axis_index_groups=groups)


def spread(block, axis, groups):
    copies = jnp.broadcast_to(block[None], (len(groups[0]),) + block.shape)
    return exchange(copies, axis, groups)


def send(block, pairs):
    return lax.ppermute(block, ALL, pairs)


def join_kernel(*refs):
    start = 0
    for piece in refs[:-1]:
        refs[-1][start : start + piece.shape[0]] = piece[...]
        start += piece.shape[0]


def forward_kernel(pieces, head_in, bias_in, hidden, slopes):
    start = 0
    for piece in pieces:
        span = slice(start, start + piece.shape[0])
        start += piece.shape[0]
        pre = jnp.dot(piece[...], head_in[...], preferred_element_type=jnp.float32) + bias_in[...]
        activated, slope = gelu_parts(pre)
        hidden[span] = activated.astype(jnp.bfloat16)
        slopes[span] = slope


def direct_kernel(head_in, bias_in, *refs):
    forward_kernel(refs[:-2], head_in, bias_in, *refs[-2:])


def late_kernel(spots, hidden_d, head_in, bias_in, head_out, *refs):
    *pieces, hidden_s, slopes_s, out = refs
    forward_kernel(pieces, head_in, bias_in, hidden_s, slopes_s)
    for part, start in ((hidden_d, 0), (hidden_s, 8)):
        share = jnp.dot(part[...], head_out[...], preferred_element_type=jnp.float32)
        for j in range(8):
            out[:, spots[start + j]] = share[64 * j : 64 * j + 64].reshape(8, 8, A)


def backward_kernel(
    spots, back, hidden_d, hidden_s, slopes_d, slopes_s, head_out, grad, bias, out, wide, rows
):
    for z in range(8):
        wide[z] = back[z].astype(jnp.float32).reshape(16, 8, A)
    for j in range(16):
        rows[64 * j : 64 * j + 64] = wide[:, spots[j]].reshape(64, A)
    bias_sum = jnp.zeros((1, A), jnp.float32)
    out_sum = jnp.zeros((A, A), jnp.float32)
    start = 0
    for hidden, slopes in ((hidden_d, slopes_d), (hidden_s, slopes_s)):
        span = slice(start, start + hidden.shape[0])
        start += hidden.shape[0]
        res = rows[span].astype(jnp.bfloat16)
        held = lax.dot_general(
            res, head_out[...], (((1,), (1,)), ((), ())), preferred_element_type=jnp.float32
        )
        rounded = (held * slopes[...]).astype(jnp.bfloat16)
        grad[span] = rounded
        bias_sum += jnp.sum(rounded.astype(jnp.float32), axis=0, keepdims=True)
        out_sum += lax.dot_general(
            hidden[...], res, (((0,), (0,)), ((), ())), preferred_element_type=jnp.float32
        )
    bias[...] = bias_sum
    out[...] = out_sum


def call(kernel, outs, operands, spots=None, scratch=()):
    vmem = pl.BlockSpec(memory_space=pltpu.VMEM)
    first = [] if spots is None else [spots]
    return pl.pallas_call(
        kernel,
        out_shape=[jax.ShapeDtypeStruct(shape, dtype) for shape, dtype in outs],
        in_specs=[pl.BlockSpec(memory_space=pltpu.SMEM)] * len(first) + [vmem] * len(operands),
        out_specs=[vmem] * len(outs),
        scratch_shapes=list(scratch),
        compiler_params=pltpu.CompilerParams(vmem_limit_bytes=20 * 1024 * 1024),
    )(*first, *operands)


def local(
    embeddings, head_in, bias_in, head_out, bias_out, block_owner, targets, entry_mask, block_mask
):
    task, fsdp = lax.axis_index("task"), lax.axis_index("fsdp")
    core, ylo = task % 2, task // 2
    x, yhi, z = fsdp // 16, fsdp // 8 % 2, fsdp % 8
    slot = fsdp // 8
    scaling = 1.0 / math.sqrt(1024)
    bf16, f32, i32 = jnp.bfloat16, jnp.float32, jnp.int32

    offset = jnp.array([d for d, _ in HELD], i32) * (1 - 2 * core)
    whose = jnp.array([w for _, w in HELD], i32)
    spots = (2 * x + yhi * 4 + ylo + 3 * z + offset + 16) % 8 * 2 + (whose + core) % 2

    measured = entry_mask.reshape(16, 8, A) * jnp.repeat(block_mask, CBLK, axis=0)[:, :, None]
    pair = jnp.stack([targets.reshape(16, 8, A), measured.astype(bf16)])
    pair = pair.transpose(2, 0, 1, 3).reshape(8, 2 * 16 * A)
    selector = (block_owner[0][:, None] == jnp.arange(8, dtype=i32)[None, :]).astype(bf16)
    pair = jnp.dot(selector, pair, preferred_element_type=f32).astype(bf16).reshape(8, 32, A)
    bias_slot = lax.dynamic_slice_in_dim(
        bias_out.reshape(8, A), lax.dynamic_index_in_dim(block_owner[0], slot, keepdims=False), 1
    )

    mine = spread(embeddings, ALL, CLASSES).reshape(64, -1)
    fourth = send(mine, from_chip(0, 1, 1))
    (both,) = call(join_kernel, [((128, mine.shape[1]), bf16)], (mine, send(mine, CORES)))
    fetched = [send(both, from_chip(*d)) for d in ((1, 0, 0), (0, 1, 0), (0, 0, 1))]
    fourth, pair = lax.optimization_barrier((fourth, pair))
    pair = exchange(pair, "fsdp", ACROSS_Z).reshape(8, 2, 16, A)
    fetched[2], pair = lax.optimization_barrier((fetched[2], pair))
    direct = [both] + fetched
    late = [send(piece, CORES) for piece in fetched] + [fourth, send(fourth, CORES)]

    r, q = jnp.arange(128, dtype=i32)[:, None], jnp.arange(128, dtype=i32)[None, :]
    row_z = (3 * (r // 16 + 32 - 2 * (z // 2) - z % 2 * 4 - r // 2 % 4)) % 8
    order = (q == r // 2 % 4 * 32 + r // 8 % 2 * 16 + row_z * 2 + r % 2).astype(bf16)
    target = jnp.dot(order, pair[:, 0].reshape(128, A), preferred_element_type=f32)
    measured = jnp.dot(order, pair[:, 1].reshape(128, A), preferred_element_type=f32)

    first, second = head_in[0], head_out[0]
    activations = [((512, A), bf16), ((512, A), f32)]
    hidden_d, slopes_d = call(direct_kernel, activations, (first, bias_in, *direct))
    hidden_s, slopes_s, shares = call(
        late_kernel,
        activations + [((8, 16, 8, A), f32)],
        (hidden_d, first, bias_in, second, *late),
        spots,
    )
    shares, direct, late = lax.optimization_barrier((shares, direct, late))
    (gathered,) = call(join_kernel, [((1024, first.shape[0]), bf16)], direct + late)
    sums = exchange(shares.reshape(8, 128, A), "fsdp", ALONG_Z).reshape(8, 128, A)
    logits = jnp.sum(sums, axis=0) + bias_slot
    residual = (measured * (logits - target) * scaling).astype(bf16)
    residual, gathered = lax.optimization_barrier((residual, gathered))
    back = spread(residual, "fsdp", ALONG_Z).reshape(8, 128, A)
    grad, bias_in_grad, head_out_grad = call(
        backward_kernel,
        [((1024, A), bf16), ((1, A), f32), ((A, A), f32)],
        (back, hidden_d, hidden_s, slopes_d, slopes_s, second),
        spots,
        [pltpu.VMEM((8, 16, 8, A), f32), pltpu.VMEM((1024, A), f32)],
    )
    head_in_grad = lax.dot_general(
        gathered, grad, (((0,), (0,)), ((), ())), preferred_element_type=f32
    )
    return head_in_grad[None], bias_in_grad, head_out_grad[None]


def solution(mesh):
    in_specs = (
        P(("task", "fsdp"), None),
        P("task", None, "fsdp"),
        P("task", "fsdp"),
        P("task", "fsdp", None),
        P("task"),
        P("task", None),
        P("fsdp", "task"),
        P("fsdp", "task"),
        P("fsdp", "task"),
    )
    out_specs = (P("task", None, "fsdp"), P("task", "fsdp"), P("task", "fsdp", None))
    return jax.shard_map(local, mesh=mesh, in_specs=in_specs, out_specs=out_specs, check_vma=False)
```

```python
import math

import jax
import jax.numpy as jnp
from jax import lax
from jax.experimental import pallas as pl
from jax.experimental.pallas import tpu as pltpu
from jax.sharding import Mesh
from jax.sharding import PartitionSpec as P

H = 1024
A = 128
CBLK = 8
TASK, FSDP = ("ylo", "core"), ("x", "yhi", "z")
ALL = TASK + FSDP

inv_root_two = 0.7071067811865476
inv_root_two_pi = 0.3989422804014327


def gelu_parts(values):
    normal_cdf = 0.5 * (1.0 + lax.erf(values * inv_root_two))
    density = jnp.exp(-0.5 * values * values) * inv_root_two_pi
    return (values * normal_cdf, normal_cdf + values * density)


def place(i):
    t, f = divmod(i, 64)
    ylo, core = divmod(t, 2)
    x, rest = divmod(f, 16)
    yhi, z = divmod(rest, 8)
    return x, yhi * 4 + ylo, z, core


def flat(x, y, z, core):
    x, y, z = x % 4, y % 8, z % 8
    return (y % 4 * 2 + core) * 64 + x * 16 + y // 4 * 8 + z


def classes():
    groups = {}
    for i in range(512):
        x, y, z, core = place(i)
        groups.setdefault(((2 * x + y + 3 * z) % 8, core), []).append(i)
    return [sorted(groups[k], key=place) for k in sorted(groups)]


def from_chip(dx, dy, dz):
    pairs = []
    for i in range(512):
        x, y, z, core = place(i)
        s = 1 - 2 * core
        pairs.append((flat(x + s * dx, y + s * dy, z + s * dz, core), i))
    return pairs


CLASSES = classes()
CORES = [(i, i ^ 64) for i in range(512)]
HELD = [(0, 0), (0, 1), (2, 0), (2, 1), (1, 0), (1, 1), (3, 0), (3, 1)]
HELD += [(-2, 1), (-2, 0), (-1, 1), (-1, 0), (-3, 1), (-3, 0), (4, 0), (4, 1)]


def exchange(blocks, axis, groups=None):
    return lax.all_to_all(blocks, axis, 0, 0, tiled=True, axis_index_groups=groups)


def spread(block, axis, count, groups=None):
    return exchange(jnp.broadcast_to(block[None], (count,) + block.shape), axis, groups)


def send(block, pairs):
    return lax.ppermute(block, ALL, pairs)


def join_kernel(*refs):
    start = 0
    for piece in refs[:-1]:
        refs[-1][start : start + piece.shape[0]] = piece[...]
        start += piece.shape[0]


def prepare_kernel(block_owner, block_mask, targets, entry_mask, out):
    row = lax.broadcasted_iota(jnp.int32, (16, A), 0)
    for b in range(8):
        o = block_owner[0, b]
        lanes = pl.ds(pl.multiple_of(o * A, A), A)
        measured = entry_mask[:, lanes] * jnp.where(row < 8, block_mask[0, o], block_mask[1, o])
        out[b, 0] = targets[:, lanes]
        out[b, 1] = measured.astype(jnp.float32).astype(jnp.bfloat16)


def gather_rows_kernel(*refs):
    *pieces, out, sems = refs
    copies, start = [], 0
    for j, piece in enumerate(pieces):
        rows = piece.shape[0]
        copies.append(pltpu.make_async_copy(piece, out.at[pl.ds(start, rows)], sems.at[j]))
        start += rows
    for copy in copies:
        copy.start()
    for copy in copies:
        copy.wait()


def residual_kernel(places, sums, pair, bias_out, out):
    owner, z = places[16], places[17]
    lanes = pl.ds(pl.multiple_of(owner * A, A), A)
    r = lax.broadcasted_iota(jnp.int32, (A, A), 0)
    q = lax.broadcasted_iota(jnp.int32, (A, A), 1)
    row_ylo = (r >> 1) & 3
    row_z = (3 * ((r >> 4) + 32 - 2 * (z >> 1) - 4 * (z & 1) - row_ylo)) & 7
    source = row_ylo * 32 + ((r >> 3) & 1) * 16 + row_z * 2 + (r & 1)
    order = jnp.where(q == source, 1.0, 0.0).astype(jnp.bfloat16)
    target = jnp.dot(
        order, pair[:, 0].reshape(A, A), preferred_element_type=jnp.float32
    )
    measured = jnp.dot(
        order, pair[:, 1].reshape(A, A), preferred_element_type=jnp.float32
    )
    total = sums[0].astype(jnp.float32)
    for j in range(1, 8):
        total = total + sums[j].astype(jnp.float32)
    logits = total + bias_out[:, lanes]
    residual = (measured * (logits - target) * (1.0 / math.sqrt(1024))).astype(jnp.bfloat16)
    for j in range(8):
        out[j] = residual


def forward_kernel(pieces, head_in, bias_in, hidden, slopes):
    start = 0
    for piece in pieces:
        span = slice(start, start + piece.shape[0])
        start += piece.shape[0]
        pre = jnp.dot(piece[...], head_in[...], preferred_element_type=jnp.float32) + bias_in[...]
        activated, slope = gelu_parts(pre)
        hidden[span] = activated.astype(jnp.bfloat16)
        slopes[span] = slope


def direct_kernel(head_in, bias_in, *refs):
    forward_kernel(refs[:-2], head_in, bias_in, *refs[-2:])


def late_kernel(spots, hidden_d, head_in, bias_in, head_out, *refs):
    *pieces, hidden_s, slopes_s, out, wide = refs
    forward_kernel(pieces, head_in, bias_in, hidden_s, slopes_s)
    for part, start in ((hidden_d, 0), (hidden_s, 8)):
        share = jnp.dot(part[...], head_out[...], preferred_element_type=jnp.float32)
        for j in range(8):
            wide[:, spots[start + j]] = share[64 * j : 64 * j + 64].reshape(8, 8, A)
    for z in range(8):
        out[z] = wide[z].reshape(A, A).astype(jnp.bfloat16)


def backward_kernel(
    spots, back, hidden_d, hidden_s, slopes_d, slopes_s, head_out, grad, bias, out, wide, rows
):
    for z in range(8):
        wide[z] = back[z].astype(jnp.float32).reshape(16, 8, A)
    for j in range(16):
        rows[64 * j : 64 * j + 64] = wide[:, spots[j]].reshape(64, A)
    bias_sum = jnp.zeros((1, A), jnp.float32)
    out_sum = jnp.zeros((A, A), jnp.float32)
    start = 0
    for hidden, slopes in ((hidden_d, slopes_d), (hidden_s, slopes_s)):
        span = slice(start, start + hidden.shape[0])
        start += hidden.shape[0]
        res = rows[span].astype(jnp.bfloat16)
        held = lax.dot_general(
            res, head_out[...], (((1,), (1,)), ((), ())), preferred_element_type=jnp.float32
        )
        rounded = (held * slopes[...]).astype(jnp.bfloat16)
        grad[span] = rounded
        bias_sum += jnp.sum(rounded.astype(jnp.float32), axis=0, keepdims=True)
        out_sum += lax.dot_general(
            hidden[...], res, (((0,), (0,)), ((), ())), preferred_element_type=jnp.float32
        )
    bias[...] = bias_sum
    out[...] = out_sum


def call(kernel, outs, operands, *scalars, scratch=()):
    vmem = pl.BlockSpec(memory_space=pltpu.VMEM)
    return pl.pallas_call(
        kernel,
        out_shape=[jax.ShapeDtypeStruct(shape, dtype) for shape, dtype in outs],
        in_specs=[pl.BlockSpec(memory_space=pltpu.SMEM)] * len(scalars) + [vmem] * len(operands),
        out_specs=[vmem] * len(outs),
        scratch_shapes=list(scratch),
        compiler_params=pltpu.CompilerParams(vmem_limit_bytes=10 * 1024 * 1024),
    )(*scalars, *operands)


def local(
    embeddings, head_in, bias_in, head_out, bias_out, block_owner, targets, entry_mask, block_mask
):
    ylo, core, x, yhi, z = [lax.axis_index(name) for name in ALL]
    bf16, f32, i32 = jnp.bfloat16, jnp.float32, jnp.int32

    offset = jnp.array([d for d, _ in HELD], i32) * (1 - 2 * core)
    whose = jnp.array([w for _, w in HELD], i32)
    spots = (2 * x + yhi * 4 + ylo + 3 * z + offset + 16) % 8 * 2 + (whose + core) % 2
    owner = lax.dynamic_index_in_dim(block_owner[0], x * 2 + yhi)
    places = jnp.concatenate([spots, owner, z[None]])

    (pair,) = call(
        prepare_kernel,
        [((8, 2, 16, A), bf16)],
        (targets, entry_mask),
        block_owner,
        block_mask,
    )
    embeddings, pair, places = lax.optimization_barrier((embeddings, pair, places))
    mine = spread(embeddings, ALL, 32, CLASSES).reshape(64, -1)
    fourth = send(mine, from_chip(0, 1, 1))
    mine, pair = lax.optimization_barrier((mine, pair))
    (both,) = call(join_kernel, [((128, mine.shape[1]), bf16)], (mine, send(mine, CORES)))
    fetched = [send(both, from_chip(*d)) for d in ((1, 0, 0), (0, 1, 0), (0, 0, 1))]
    direct = [both] + fetched
    late = [send(piece, CORES) for piece in fetched] + [fourth, send(fourth, CORES)]

    first, second = head_in[0], head_out[0]
    activations = [((512, A), bf16), ((512, A), f32)]
    hidden_d, slopes_d = call(direct_kernel, activations, (first, bias_in, *direct))
    hidden_s, slopes_s, shares = call(
        late_kernel,
        activations + [((8, A, A), bf16)],
        (hidden_d, first, bias_in, second, *late),
        places,
        scratch=[pltpu.VMEM((8, 16, 8, A), f32)],
    )
    shares, direct, late = lax.optimization_barrier((shares, direct, late))
    pair = exchange(pair, ("x", "yhi"))
    held = direct + late
    gathered = pl.pallas_call(
        gather_rows_kernel,
        out_shape=jax.ShapeDtypeStruct((1024, first.shape[0]), bf16),
        in_specs=[pl.BlockSpec(memory_space=pl.ANY)] * len(held),
        out_specs=pl.BlockSpec(memory_space=pl.ANY),
        scratch_shapes=[pltpu.SemaphoreType.DMA((len(held),))],
        compiler_params=pltpu.CompilerParams(vmem_limit_bytes=2 * 1024 * 1024),
    )(*held)
    sums = exchange(shares, "z")
    (copies,) = call(
        residual_kernel, [((8, A, A), bf16)], (sums, pair, bias_out[None]), places
    )
    copies, gathered = lax.optimization_barrier((copies, gathered))
    back = exchange(copies, "z")
    grad, bias_in_grad, head_out_grad = call(
        backward_kernel,
        [((1024, A), bf16), ((1, A), f32), ((A, A), f32)],
        (back, hidden_d, hidden_s, slopes_d, slopes_s, second),
        places,
        scratch=[pltpu.VMEM((8, 16, 8, A), f32), pltpu.VMEM((1024, A), f32)],
    )
    head_in_grad = lax.dot_general(
        gathered, grad, (((0,), (0,)), ((), ())), preferred_element_type=f32
    )
    return head_in_grad[None], bias_in_grad, head_out_grad[None]


def solution(mesh):
    mesh = Mesh(mesh.devices.reshape(4, 2, 4, 2, 8), ALL)
    in_specs = (
        P(ALL, None),
        P(TASK, None, FSDP),
        P(TASK, FSDP),
        P(TASK, FSDP, None),
        P(TASK),
        P(TASK, None),
        P(FSDP, TASK),
        P(FSDP, TASK),
        P(FSDP, TASK),
    )
    out_specs = (P(TASK, None, FSDP), P(TASK, FSDP), P(TASK, FSDP, None))
    return jax.shard_map(local, mesh=mesh, in_specs=in_specs, out_specs=out_specs, check_vma=False)
```

```python
import math

import jax
import jax.numpy as jnp
from jax import lax
from jax.experimental import pallas as pl
from jax.experimental.pallas import tpu as pltpu
from jax.sharding import Mesh
from jax.sharding import PartitionSpec as P

H = 1024
A = 128
KEPT = pltpu.HBM
TASK, FSDP = ("ylo", "core"), ("x", "yhi", "z")
ALL = TASK + FSDP

inv_root_two = 0.7071067811865476
inv_root_two_pi = 0.3989422804014327


def gelu_parts(values):
    normal_cdf = 0.5 * (1.0 + lax.erf(values * inv_root_two))
    density = jnp.exp(-0.5 * values * values) * inv_root_two_pi
    return (values * normal_cdf, normal_cdf + values * density)


def place(i):
    t, f = divmod(i, 64)
    ylo, core = divmod(t, 2)
    x, rest = divmod(f, 16)
    yhi, z = divmod(rest, 8)
    return x, yhi * 4 + ylo, z, core


def flat(x, y, z, core):
    x, y, z = x % 4, y % 8, z % 8
    return (y % 4 * 2 + core) * 64 + x * 16 + y // 4 * 8 + z


def classes():
    groups = {}
    for i in range(512):
        x, y, z, core = place(i)
        groups.setdefault(((2 * x + y + 3 * z) % 8, core), []).append(i)
    return [sorted(groups[k], key=place) for k in sorted(groups)]


def from_chip(dx, dy, dz):
    pairs = []
    for i in range(512):
        x, y, z, core = place(i)
        s = 1 - 2 * core
        pairs.append((flat(x + s * dx, y + s * dy, z + s * dz, core), i))
    return pairs


CLASSES = classes()
CORES = [(i, i ^ 64) for i in range(512)]
HELD = [(0, 0), (0, 1), (2, 0), (2, 1), (1, 0), (1, 1), (3, 0), (3, 1)]
HELD += [(-2, 1), (-2, 0), (-1, 1), (-1, 0), (-3, 1), (-3, 0), (4, 0), (4, 1)]


def exchange(blocks, axis, groups=None):
    return lax.all_to_all(blocks, axis, 0, 0, tiled=True, axis_index_groups=groups)


def spread(block, axis, count, groups=None):
    return exchange(jnp.broadcast_to(block[None], (count,) + block.shape), axis, groups)


def send(block, pairs):
    return lax.ppermute(block, ALL, pairs)


def join_kernel(*refs):
    start = 0
    for piece in refs[:-1]:
        refs[-1][start : start + piece.shape[0]] = piece[...]
        start += piece.shape[0]


def prepare_kernel(block_owner, block_mask, targets, entry_mask, out):
    row = lax.broadcasted_iota(jnp.int32, (16, A), 0)
    for b in range(8):
        o = block_owner[0, b]
        lanes = pl.ds(pl.multiple_of(o * A, A), A)
        measured = entry_mask[:, lanes] * jnp.where(row < 8, block_mask[0, o], block_mask[1, o])
        out[b, 0] = targets[:, lanes]
        out[b, 1] = measured.astype(jnp.float32).astype(jnp.bfloat16)


def last_kernel(*refs):
    *pieces, grad, out, held, sems = refs
    width = held.shape[2]

    def copies(step):
        slot, start, made = step % 2, 0, []
        for j, piece in enumerate(pieces):
            rows = piece.shape[0]
            source = piece.at[:, pl.ds(step * width, width)]
            target = held.at[slot, pl.ds(start, rows)]
            made.append(pltpu.make_async_copy(source, target, sems.at[slot, j]))
            start += rows
        return made

    steps = out.shape[0] // width
    for step in range(2):
        for copy in copies(step):
            copy.start()
    weights = grad[...]
    for step in range(steps):
        for copy in copies(step):
            copy.wait()
        product = lax.dot_general(
            weights, held[step % 2], (((0,), (0,)), ((), ())), preferred_element_type=jnp.float32
        )
        out[step * width : step * width + width] = product.T
        if step + 2 < steps:
            for copy in copies(step + 2):
                copy.start()


def residual_kernel(places, sums, pair, bias_out, out):
    owner, z = places[16], places[17]
    lanes = pl.ds(pl.multiple_of(owner * A, A), A)
    r = lax.broadcasted_iota(jnp.int32, (A, A), 0)
    q = lax.broadcasted_iota(jnp.int32, (A, A), 1)
    row_ylo = (r >> 1) & 3
    row_z = (3 * ((r >> 4) + 32 - 2 * (z >> 1) - 4 * (z & 1) - row_ylo)) & 7
    source = row_ylo * 32 + ((r >> 3) & 1) * 16 + row_z * 2 + (r & 1)
    order = jnp.where(q == source, 1.0, 0.0).astype(jnp.bfloat16)
    target = jnp.dot(
        order, pair[:, 0].reshape(A, A), preferred_element_type=jnp.float32
    )
    measured = jnp.dot(
        order, pair[:, 1].reshape(A, A), preferred_element_type=jnp.float32
    )
    total = sums[0].astype(jnp.float32)
    for j in range(1, 8):
        total = total + sums[j].astype(jnp.float32)
    logits = total + bias_out[:, lanes]
    residual = (measured * (logits - target) * (1.0 / math.sqrt(1024))).astype(jnp.bfloat16)
    for j in range(8):
        out[j] = residual


def forward_kernel(pieces, head_in, bias_in, hidden, slopes):
    start = 0
    for piece in pieces:
        span = slice(start, start + piece.shape[0])
        start += piece.shape[0]
        pre = jnp.dot(piece[...], head_in[...], preferred_element_type=jnp.float32) + bias_in[...]
        activated, slope = gelu_parts(pre)
        hidden[span] = activated.astype(jnp.bfloat16)
        slopes[span] = slope


def direct_kernel(head_in, bias_in, *refs):
    forward_kernel(refs[:-2], head_in, bias_in, *refs[-2:])


def late_kernel(spots, hidden_d, head_in, bias_in, head_out, *refs):
    *pieces, hidden_s, slopes_s, out, wide = refs
    forward_kernel(pieces, head_in, bias_in, hidden_s, slopes_s)
    for part, start in ((hidden_d, 0), (hidden_s, 8)):
        share = jnp.dot(part[...], head_out[...], preferred_element_type=jnp.float32)
        for j in range(8):
            wide[:, spots[start + j]] = share[64 * j : 64 * j + 64].reshape(8, 8, A)
    for z in range(8):
        out[z] = wide[z].reshape(A, A).astype(jnp.bfloat16)


def backward_kernel(
    spots, back, hidden_d, hidden_s, slopes_d, slopes_s, head_out, grad, bias, out, wide, rows
):
    for z in range(8):
        wide[z] = back[z].astype(jnp.float32).reshape(16, 8, A)
    for j in range(16):
        rows[64 * j : 64 * j + 64] = wide[:, spots[j]].reshape(64, A)
    bias_sum = jnp.zeros((1, A), jnp.float32)
    out_sum = jnp.zeros((A, A), jnp.float32)
    start = 0
    for hidden, slopes in ((hidden_d, slopes_d), (hidden_s, slopes_s)):
        span = slice(start, start + hidden.shape[0])
        start += hidden.shape[0]
        res = rows[span].astype(jnp.bfloat16)
        held = lax.dot_general(
            res, head_out[...], (((1,), (1,)), ((), ())), preferred_element_type=jnp.float32
        )
        rounded = (held * slopes[...]).astype(jnp.bfloat16)
        grad[span] = rounded
        bias_sum += jnp.sum(rounded.astype(jnp.float32), axis=0, keepdims=True)
        out_sum += lax.dot_general(
            hidden[...], res, (((0,), (0,)), ((), ())), preferred_element_type=jnp.float32
        )
    bias[...] = bias_sum
    out[...] = out_sum


def hbm(*arrays):
    return [pltpu.with_memory_space_constraint(array, pltpu.HBM) for array in arrays]


def call(kernel, outs, operands, *scalars, scratch=()):
    vmem = pl.BlockSpec(memory_space=pltpu.VMEM)
    return pl.pallas_call(
        kernel,
        out_shape=outs,
        in_specs=[pl.BlockSpec(memory_space=pltpu.SMEM)] * len(scalars) + [vmem] * len(operands),
        out_specs=[vmem] * len(outs),
        scratch_shapes=list(scratch),
        compiler_params=pltpu.CompilerParams(vmem_limit_bytes=12 * 1024 * 1024),
    )(*scalars, *operands)


def local(
    embeddings, head_in, bias_in, head_out, bias_out, block_owner, targets, entry_mask, block_mask
):
    ylo, core, x, yhi, z = [lax.axis_index(name) for name in ALL]
    bf16, f32, i32 = jnp.bfloat16, jnp.float32, jnp.int32

    offset = jnp.array([d for d, _ in HELD], i32) * (1 - 2 * core)
    whose = jnp.array([w for _, w in HELD], i32)
    spots = (2 * x + yhi * 4 + ylo + 3 * z + offset + 16) % 8 * 2 + (whose + core) % 2
    owner = lax.dynamic_index_in_dim(block_owner[0], x * 2 + yhi)
    places = jnp.concatenate([spots, owner, z[None]])

    def whole(shape, dtype=bf16):
        return jax.ShapeDtypeStruct(shape, dtype)

    (pair,) = call(
        prepare_kernel,
        [whole((8, 2, 16, A))],
        (targets, entry_mask),
        block_owner,
        block_mask,
    )
    mine = spread(embeddings, ALL, 32, CLASSES).reshape(64, -1)
    mine, pair, places = lax.optimization_barrier((mine, pair, places))
    fourth = send(mine, from_chip(0, 1, 1))
    (both,) = call(join_kernel, [whole((128, mine.shape[1]))], (mine, send(mine, CORES)))
    fetched = [send(both, from_chip(*d)) for d in ((1, 0, 0), (0, 1, 0), (0, 0, 1))]
    direct = [both] + fetched
    late = [send(piece, CORES) for piece in fetched] + [fourth, send(fourth, CORES)]
    pair = exchange(pair, ("x", "yhi"))

    first, second = head_in[0], head_out[0]
    first_held, bias_held, second_held = hbm(first, bias_in, second)
    activations = [KEPT((512, A), bf16), KEPT((512, A), f32)]
    hidden_d, slopes_d = call(direct_kernel, activations, (first_held, bias_held, *direct))
    hidden_s, slopes_s, shares = call(
        late_kernel,
        activations + [KEPT((8, A, A), bf16)],
        (*hbm(hidden_d), first_held, bias_held, second_held, *late),
        places,
        scratch=[pltpu.VMEM((8, 16, 8, A), f32)],
    )
    sums = exchange(shares, "z")
    (copies,) = call(
        residual_kernel, [whole((8, A, A))], (sums, pair, *hbm(bias_out[None])), places
    )
    back = exchange(copies, "z")
    grad, bias_in_grad, head_out_grad = call(
        backward_kernel,
        [whole((1024, A)), whole((1, A), f32), whole((A, A), f32)],
        (back, *hbm(hidden_d, hidden_s, slopes_d, slopes_s, second)),
        places,
        scratch=[pltpu.VMEM((8, 16, 8, A), f32), pltpu.VMEM((1024, A), f32)],
    )
    held = direct + late
    any_space, vmem = pl.BlockSpec(memory_space=pl.ANY), pl.BlockSpec(memory_space=pltpu.VMEM)
    head_in_grad = pl.pallas_call(
        last_kernel,
        out_shape=whole((first.shape[0], A), f32),
        in_specs=[any_space] * len(held) + [vmem],
        out_specs=vmem,
        scratch_shapes=[
            pltpu.VMEM((2, 1024, 1024), bf16),
            pltpu.SemaphoreType.DMA((2, len(held))),
        ],
        compiler_params=pltpu.CompilerParams(vmem_limit_bytes=20 * 1024 * 1024),
    )(*held, grad)
    return head_in_grad[None], bias_in_grad, head_out_grad[None]


def solution(mesh):
    mesh = Mesh(mesh.devices.reshape(4, 2, 4, 2, 8), ALL)
    in_specs = (
        P(ALL, None),
        P(TASK, None, FSDP),
        P(TASK, FSDP),
        P(TASK, FSDP, None),
        P(TASK),
        P(TASK, None),
        P(FSDP, TASK),
        P(FSDP, TASK),
        P(FSDP, TASK),
    )
    out_specs = (P(TASK, None, FSDP), P(TASK, FSDP), P(TASK, FSDP, None))
    return jax.shard_map(local, mesh=mesh, in_specs=in_specs, out_specs=out_specs, check_vma=False)
```

```python
import math

import jax
import jax.numpy as jnp
from jax import lax
from jax.experimental import pallas as pl
from jax.experimental.pallas import tpu as pltpu
from jax.sharding import Mesh
from jax.sharding import PartitionSpec as P

H = 1024
A = 128
KEPT = pltpu.HBM
TASK, FSDP = ("ylo", "core"), ("x", "yhi", "z")
ALL = TASK + FSDP

inv_root_two = 0.7071067811865476
inv_root_two_pi = 0.3989422804014327


def gelu_parts(values):
    normal_cdf = 0.5 * (1.0 + lax.erf(values * inv_root_two))
    density = jnp.exp(-0.5 * values * values) * inv_root_two_pi
    return (values * normal_cdf, normal_cdf + values * density)


def place(i):
    t, f = divmod(i, 64)
    ylo, core = divmod(t, 2)
    x, rest = divmod(f, 16)
    yhi, z = divmod(rest, 8)
    return x, yhi * 4 + ylo, z, core


def flat(x, y, z, core):
    x, y, z = x % 4, y % 8, z % 8
    return (y % 4 * 2 + core) * 64 + x * 16 + y // 4 * 8 + z


def classes():
    groups = {}
    for i in range(512):
        x, y, z, core = place(i)
        groups.setdefault(((2 * x + y + 3 * z) % 8, core), []).append(i)
    return [sorted(groups[k], key=place) for k in sorted(groups)]


def from_chip(dx, dy, dz):
    pairs = []
    for i in range(512):
        x, y, z, core = place(i)
        s = 1 - 2 * core
        pairs.append((flat(x + s * dx, y + s * dy, z + s * dz, core), i))
    return pairs


CLASSES = classes()
CORES = [(i, i ^ 64) for i in range(512)]
HELD = [(0, 0), (0, 1), (2, 0), (2, 1), (1, 0), (1, 1), (3, 0), (3, 1)]
HELD += [(-2, 1), (-2, 0), (-1, 1), (-1, 0), (-3, 1), (-3, 0), (4, 0), (4, 1)]


def exchange(blocks, axis, groups=None):
    return lax.all_to_all(blocks, axis, 0, 0, tiled=True, axis_index_groups=groups)


def spread(block, axis, count, groups=None):
    return exchange(jnp.broadcast_to(block[None], (count,) + block.shape), axis, groups)


def send(block, pairs):
    return lax.ppermute(block, ALL, pairs)


def join_kernel(*refs):
    start = 0
    for piece in refs[:-1]:
        refs[-1][start : start + piece.shape[0]] = piece[...]
        start += piece.shape[0]


def prepare_kernel(block_owner, block_mask, targets, entry_mask, out):
    row = lax.broadcasted_iota(jnp.int32, (16, A), 0)
    for b in range(8):
        o = block_owner[0, b]
        lanes = pl.ds(pl.multiple_of(o * A, A), A)
        measured = entry_mask[:, lanes] * jnp.where(row < 8, block_mask[0, o], block_mask[1, o])
        out[b, 0] = targets[:, lanes]
        out[b, 1] = measured.astype(jnp.float32).astype(jnp.bfloat16)


def residual_kernel(places, sums, pair, bias_out, out):
    owner, z = places[16], places[17]
    lanes = pl.ds(pl.multiple_of(owner * A, A), A)
    r = lax.broadcasted_iota(jnp.int32, (A, A), 0)
    q = lax.broadcasted_iota(jnp.int32, (A, A), 1)
    row_ylo = (r >> 1) & 3
    row_z = (3 * ((r >> 4) + 32 - 2 * (z >> 1) - 4 * (z & 1) - row_ylo)) & 7
    source = row_ylo * 32 + ((r >> 3) & 1) * 16 + row_z * 2 + (r & 1)
    order = jnp.where(q == source, 1.0, 0.0).astype(jnp.bfloat16)
    target = jnp.dot(
        order, pair[:, 0].reshape(A, A), preferred_element_type=jnp.float32
    )
    measured = jnp.dot(
        order, pair[:, 1].reshape(A, A), preferred_element_type=jnp.float32
    )
    total = sums[0].astype(jnp.float32)
    for j in range(1, 8):
        total = total + sums[j].astype(jnp.float32)
    logits = total + bias_out[:, lanes]
    residual = (measured * (logits - target) * (1.0 / math.sqrt(1024))).astype(jnp.bfloat16)
    for j in range(8):
        out[j] = residual


def forward_kernel(pieces, head_in, bias_in, hidden, slopes, held, weights, sems):
    copies = [pltpu.make_async_copy(head_in, weights, sems.at[0])]
    spans, start = [], 0
    for j, piece in enumerate(pieces):
        rows = piece.shape[0]
        target = held.at[pl.ds(start, rows)]
        copies.append(pltpu.make_async_copy(piece, target, sems.at[j + 1]))
        spans.append(slice(start, start + rows))
        start += rows
    for copy in copies:
        copy.start()
    copies[0].wait()
    for span, copy in zip(spans, copies[1:]):
        copy.wait()
        pre = jnp.dot(held[span], weights[...], preferred_element_type=jnp.float32) + bias_in[...]
        activated, slope = gelu_parts(pre)
        hidden[span] = activated.astype(jnp.bfloat16)
        slopes[span] = slope


def direct_kernel(bias_in, head_in, *refs):
    *pieces, hidden, slopes, held, weights, sems = refs
    forward_kernel(pieces, head_in, bias_in, hidden, slopes, held, weights, sems)


def late_kernel(spots, hidden_d, bias_in, head_out, head_in, *refs):
    *pieces, hidden_s, slopes_s, out, held, weights, sems, wide = refs
    forward_kernel(pieces, head_in, bias_in, hidden_s, slopes_s, held, weights, sems)
    for part, start in ((hidden_d, 0), (hidden_s, 8)):
        share = jnp.dot(part[...], head_out[...], preferred_element_type=jnp.float32)
        for j in range(8):
            wide[:, spots[start + j]] = share[64 * j : 64 * j + 64].reshape(8, 8, A)
    for z in range(8):
        out[z] = wide[z].reshape(A, A).astype(jnp.bfloat16)


def backward_kernel(
    spots, back, hidden_d, hidden_s, slopes_d, slopes_s, head_out, grad, bias, out, wide, rows
):
    for z in range(8):
        wide[z] = back[z].astype(jnp.float32).reshape(16, 8, A)
    for j in range(16):
        rows[64 * j : 64 * j + 64] = wide[:, spots[j]].reshape(64, A)
    bias_sum = jnp.zeros((1, A), jnp.float32)
    out_sum = jnp.zeros((A, A), jnp.float32)
    start = 0
    for hidden, slopes in ((hidden_d, slopes_d), (hidden_s, slopes_s)):
        span = slice(start, start + hidden.shape[0])
        start += hidden.shape[0]
        res = rows[span].astype(jnp.bfloat16)
        held = lax.dot_general(
            res, head_out[...], (((1,), (1,)), ((), ())), preferred_element_type=jnp.float32
        )
        rounded = (held * slopes[...]).astype(jnp.bfloat16)
        grad[span] = rounded
        bias_sum += jnp.sum(rounded.astype(jnp.float32), axis=0, keepdims=True)
        out_sum += lax.dot_general(
            hidden[...], res, (((0,), (0,)), ((), ())), preferred_element_type=jnp.float32
        )
    bias[...] = bias_sum
    out[...] = out_sum


def last_kernel(spots, back, hidden_d, hidden_s, slopes_d, slopes_s, head_out, *refs):
    *pieces, bias, head_out_grad, out, wide, rows, grad, held, sems = refs
    width = held.shape[2]

    def copies(step):
        slot, start, made = step % 2, 0, []
        for j, piece in enumerate(pieces):
            count = piece.shape[0]
            source = piece.at[:, pl.ds(step * width, width)]
            target = held.at[slot, pl.ds(start, count)]
            made.append(pltpu.make_async_copy(source, target, sems.at[slot, j]))
            start += count
        return made

    steps = out.shape[0] // width
    for step in range(2):
        for copy in copies(step):
            copy.start()
    backward_kernel(
        spots, back, hidden_d, hidden_s, slopes_d, slopes_s, head_out, grad, bias, head_out_grad,
        wide, rows,
    )
    weights = grad[...]
    for step in range(steps):
        for copy in copies(step):
            copy.wait()
        product = lax.dot_general(
            weights, held[step % 2], (((0,), (0,)), ((), ())), preferred_element_type=jnp.float32
        )
        out[step * width : step * width + width] = product.T
        if step + 2 < steps:
            for copy in copies(step + 2):
                copy.start()


def hbm(*arrays):
    return [pltpu.with_memory_space_constraint(array, pltpu.HBM) for array in arrays]


def call(kernel, outs, operands, *scalars, fetched=(), scratch=(), limit=12):
    vmem, anywhere = pl.BlockSpec(memory_space=pltpu.VMEM), pl.BlockSpec(memory_space=pl.ANY)
    smem = pl.BlockSpec(memory_space=pltpu.SMEM)
    return pl.pallas_call(
        kernel,
        out_shape=outs,
        in_specs=[smem] * len(scalars) + [vmem] * len(operands) + [anywhere] * len(fetched),
        out_specs=[vmem] * len(outs),
        scratch_shapes=list(scratch),
        compiler_params=pltpu.CompilerParams(vmem_limit_bytes=limit * 1024 * 1024),
    )(*scalars, *operands, *fetched)


def local(
    embeddings, head_in, bias_in, head_out, bias_out, block_owner, targets, entry_mask, block_mask
):
    ylo, core, x, yhi, z = [lax.axis_index(name) for name in ALL]
    bf16, f32, i32 = jnp.bfloat16, jnp.float32, jnp.int32

    offset = jnp.array([d for d, _ in HELD], i32) * (1 - 2 * core)
    whose = jnp.array([w for _, w in HELD], i32)
    spots = (2 * x + yhi * 4 + ylo + 3 * z + offset + 16) % 8 * 2 + (whose + core) % 2
    owner = lax.dynamic_index_in_dim(block_owner[0], x * 2 + yhi)
    places = jnp.concatenate([spots, owner, z[None]])

    def whole(shape, dtype=bf16):
        return jax.ShapeDtypeStruct(shape, dtype)

    (pair,) = call(
        prepare_kernel,
        [whole((8, 2, 16, A))],
        (targets, entry_mask),
        block_owner,
        block_mask,
    )
    mine = spread(embeddings, ALL, 32, CLASSES).reshape(64, -1)
    mine, pair, places = lax.optimization_barrier((mine, pair, places))
    fourth = send(mine, from_chip(0, 1, 1))
    (both,) = call(join_kernel, [whole((128, mine.shape[1]))], (mine, send(mine, CORES)))
    fetched = [send(both, from_chip(*d)) for d in ((1, 0, 0), (0, 1, 0), (0, 0, 1))]
    direct = [both] + fetched
    pair, both = lax.optimization_barrier((pair, both))
    pair = exchange(pair, ("x", "yhi"))
    fetched[0], pair = lax.optimization_barrier((fetched[0], pair))
    late = [send(piece, CORES) for piece in fetched] + [fourth, send(fourth, CORES)]

    first, second = head_in[0], head_out[0]
    first_held, bias_held, second_held = hbm(first, bias_in, second)
    activations = [KEPT((512, A), bf16), KEPT((512, A), f32)]
    width = first.shape[0]
    landing = [
        pltpu.VMEM((512, width), bf16),
        pltpu.VMEM((width, A), bf16),
        pltpu.SemaphoreType.DMA((6,)),
    ]
    hidden_d, slopes_d = call(
        direct_kernel, activations, (bias_held,), fetched=(first_held, *direct), scratch=landing
    )
    hidden_s, slopes_s, shares = call(
        late_kernel,
        activations + [KEPT((8, A, A), bf16)],
        (*hbm(hidden_d), bias_held, second_held),
        places,
        fetched=(first_held, *late),
        scratch=landing + [pltpu.VMEM((8, 16, 8, A), f32)],
    )
    sums = exchange(shares, "z")
    (copies,) = call(
        residual_kernel, [whole((8, A, A))], (sums, pair, *hbm(bias_out[None])), places
    )
    back = exchange(copies, "z")
    bias_in_grad, head_out_grad, head_in_grad = call(
        last_kernel,
        [whole((1, A), f32), whole((A, A), f32), whole((width, A), f32)],
        (back, *hbm(hidden_d, hidden_s, slopes_d, slopes_s, second)),
        places,
        fetched=direct + late,
        scratch=[
            pltpu.VMEM((8, 16, 8, A), f32),
            pltpu.VMEM((1024, A), f32),
            pltpu.VMEM((1024, A), bf16),
            pltpu.VMEM((2, 1024, 1024), bf16),
            pltpu.SemaphoreType.DMA((2, 9)),
        ],
        limit=20,
    )
    return head_in_grad[None], bias_in_grad, head_out_grad[None]


def solution(mesh):
    mesh = Mesh(mesh.devices.reshape(4, 2, 4, 2, 8), ALL)
    in_specs = (
        P(ALL, None),
        P(TASK, None, FSDP),
        P(TASK, FSDP),
        P(TASK, FSDP, None),
        P(TASK),
        P(TASK, None),
        P(FSDP, TASK),
        P(FSDP, TASK),
        P(FSDP, TASK),
    )
    out_specs = (P(TASK, None, FSDP), P(TASK, FSDP), P(TASK, FSDP, None))
    return jax.shard_map(local, mesh=mesh, in_specs=in_specs, out_specs=out_specs, check_vma=False)
```

```python
import math

import jax
import jax.numpy as jnp
from jax import lax
from jax.experimental import pallas as pl
from jax.experimental.pallas import tpu as pltpu
from jax.sharding import Mesh
from jax.sharding import PartitionSpec as P

H = 1024
A = 128
KEPT = pltpu.HBM
TASK, FSDP = ("ylo", "core"), ("x", "yhi", "z")
ALL = TASK + FSDP

inv_root_two = 0.7071067811865476
inv_root_two_pi = 0.3989422804014327


def gelu_parts(values):
    normal_cdf = 0.5 * (1.0 + lax.erf(values * inv_root_two))
    density = jnp.exp(-0.5 * values * values) * inv_root_two_pi
    return (values * normal_cdf, normal_cdf + values * density)


def place(i):
    t, f = divmod(i, 64)
    ylo, core = divmod(t, 2)
    x, rest = divmod(f, 16)
    yhi, z = divmod(rest, 8)
    return x, yhi * 4 + ylo, z, core


def flat(x, y, z, core):
    x, y, z = x % 4, y % 8, z % 8
    return (y % 4 * 2 + core) * 64 + x * 16 + y // 4 * 8 + z


def classes():
    groups = {}
    for i in range(512):
        x, y, z, core = place(i)
        groups.setdefault(((2 * x + y + 3 * z) % 8, core), []).append(i)
    return [sorted(groups[k], key=place) for k in sorted(groups)]


def from_chip(dx, dy, dz):
    pairs = []
    for i in range(512):
        x, y, z, core = place(i)
        s = 1 - 2 * core
        pairs.append((flat(x + s * dx, y + s * dy, z + s * dz, core), i))
    return pairs


CLASSES = classes()
CORES = [(i, i ^ 64) for i in range(512)]
HELD = [(0, 0), (0, 1), (2, 0), (2, 1), (1, 0), (1, 1), (3, 0), (3, 1)]
HELD += [(-2, 1), (-2, 0), (-1, 1), (-1, 0), (-3, 1), (-3, 0), (4, 0), (4, 1)]


def exchange(blocks, axis, groups=None):
    return lax.all_to_all(blocks, axis, 0, 0, tiled=True, axis_index_groups=groups)


def spread(block, axis, count, groups=None):
    return exchange(jnp.broadcast_to(block[None], (count,) + block.shape), axis, groups)


def send(block, pairs):
    return lax.ppermute(block, ALL, pairs)


def join_kernel(*refs):
    start = 0
    for piece in refs[:-1]:
        refs[-1][start : start + piece.shape[0]] = piece[...]
        start += piece.shape[0]


def prepare_kernel(block_owner, block_mask, targets, entry_mask, out):
    row = lax.broadcasted_iota(jnp.int32, (16, A), 0)
    for b in range(8):
        o = block_owner[0, b]
        lanes = pl.ds(pl.multiple_of(o * A, A), A)
        measured = entry_mask[:, lanes] * jnp.where(row < 8, block_mask[0, o], block_mask[1, o])
        out[b, 0] = targets[:, lanes]
        out[b, 1] = measured.astype(jnp.float32).astype(jnp.bfloat16)


def residual_kernel(places, sums, pair, bias_out, out):
    owner, z = places[16], places[17]
    lanes = pl.ds(pl.multiple_of(owner * A, A), A)
    r = lax.broadcasted_iota(jnp.int32, (A, A), 0)
    q = lax.broadcasted_iota(jnp.int32, (A, A), 1)
    row_ylo = (r >> 1) & 3
    row_z = (3 * ((r >> 4) + 32 - 2 * (z >> 1) - 4 * (z & 1) - row_ylo)) & 7
    source = row_ylo * 32 + ((r >> 3) & 1) * 16 + row_z * 2 + (r & 1)
    order = jnp.where(q == source, 1.0, 0.0).astype(jnp.bfloat16)
    target = jnp.dot(
        order, pair[:, 0].reshape(A, A), preferred_element_type=jnp.float32
    )
    measured = jnp.dot(
        order, pair[:, 1].reshape(A, A), preferred_element_type=jnp.float32
    )
    total = sums[0].astype(jnp.float32)
    for j in range(1, 8):
        total = total + sums[j].astype(jnp.float32)
    logits = total + bias_out[:, lanes]
    residual = (measured * (logits - target) * (1.0 / math.sqrt(1024))).astype(jnp.bfloat16)
    for j in range(8):
        out[j] = residual


def forward_kernel(pieces, head_in, bias_in, hidden, slopes):
    start = 0
    for piece in pieces:
        span = slice(start, start + piece.shape[0])
        start += piece.shape[0]
        pre = jnp.dot(piece[...], head_in[...], preferred_element_type=jnp.float32) + bias_in[...]
        activated, slope = gelu_parts(pre)
        hidden[span] = activated.astype(jnp.bfloat16)
        slopes[span] = slope


def direct_kernel(head_in, bias_in, *refs):
    forward_kernel(refs[:-2], head_in, bias_in, *refs[-2:])


def late_kernel(spots, hidden_d, head_in, bias_in, head_out, *refs):
    *pieces, hidden_s, slopes_s, out, wide = refs
    forward_kernel(pieces, head_in, bias_in, hidden_s, slopes_s)
    for part, start in ((hidden_d, 0), (hidden_s, 8)):
        share = jnp.dot(part[...], head_out[...], preferred_element_type=jnp.float32)
        for j in range(8):
            wide[:, spots[start + j]] = share[64 * j : 64 * j + 64].reshape(8, 8, A)
    for z in range(8):
        out[z] = wide[z].reshape(A, A).astype(jnp.bfloat16)


def backward_kernel(
    spots, back, hidden_d, hidden_s, slopes_d, slopes_s, head_out, grad, bias, out, wide, rows
):
    for z in range(8):
        wide[z] = back[z].astype(jnp.float32).reshape(16, 8, A)
    for j in range(16):
        rows[64 * j : 64 * j + 64] = wide[:, spots[j]].reshape(64, A)
    bias_sum = jnp.zeros((1, A), jnp.float32)
    out_sum = jnp.zeros((A, A), jnp.float32)
    start = 0
    for hidden, slopes in ((hidden_d, slopes_d), (hidden_s, slopes_s)):
        span = slice(start, start + hidden.shape[0])
        start += hidden.shape[0]
        res = rows[span].astype(jnp.bfloat16)
        held = lax.dot_general(
            res, head_out[...], (((1,), (1,)), ((), ())), preferred_element_type=jnp.float32
        )
        rounded = (held * slopes[...]).astype(jnp.bfloat16)
        grad[span] = rounded
        bias_sum += jnp.sum(rounded.astype(jnp.float32), axis=0, keepdims=True)
        out_sum += lax.dot_general(
            hidden[...], res, (((0,), (0,)), ((), ())), preferred_element_type=jnp.float32
        )
    bias[...] = bias_sum
    out[...] = out_sum


def last_kernel(spots, back, hidden_d, hidden_s, slopes_d, slopes_s, head_out, *refs):
    *pieces, bias, head_out_grad, out, wide, rows, grad, held, sems = refs
    width = held.shape[2]

    def copies(step):
        slot, start, made = step % 2, 0, []
        for j, piece in enumerate(pieces):
            count = piece.shape[0]
            source = piece.at[:, pl.ds(step * width, width)]
            target = held.at[slot, pl.ds(start, count)]
            made.append(pltpu.make_async_copy(source, target, sems.at[slot, j]))
            start += count
        return made

    steps = out.shape[0] // width
    for step in range(2):
        for copy in copies(step):
            copy.start()
    backward_kernel(
        spots, back, hidden_d, hidden_s, slopes_d, slopes_s, head_out, grad, bias, head_out_grad,
        wide, rows,
    )
    weights = grad[...]
    for step in range(steps):
        for copy in copies(step):
            copy.wait()
        product = lax.dot_general(
            weights, held[step % 2], (((0,), (0,)), ((), ())), preferred_element_type=jnp.float32
        )
        out[step * width : step * width + width] = product.T
        if step + 2 < steps:
            for copy in copies(step + 2):
                copy.start()


def hbm(*arrays):
    return [pltpu.with_memory_space_constraint(array, pltpu.HBM) for array in arrays]


def call(kernel, outs, operands, *scalars, fetched=(), scratch=(), limit=12):
    vmem, anywhere = pl.BlockSpec(memory_space=pltpu.VMEM), pl.BlockSpec(memory_space=pl.ANY)
    smem = pl.BlockSpec(memory_space=pltpu.SMEM)
    return pl.pallas_call(
        kernel,
        out_shape=outs,
        in_specs=[smem] * len(scalars) + [vmem] * len(operands) + [anywhere] * len(fetched),
        out_specs=[vmem] * len(outs),
        scratch_shapes=list(scratch),
        compiler_params=pltpu.CompilerParams(vmem_limit_bytes=limit * 1024 * 1024),
    )(*scalars, *operands, *fetched)


def local(
    embeddings, head_in, bias_in, head_out, bias_out, block_owner, targets, entry_mask, block_mask
):
    ylo, core, x, yhi, z = [lax.axis_index(name) for name in ALL]
    bf16, f32, i32 = jnp.bfloat16, jnp.float32, jnp.int32

    offset = jnp.array([d for d, _ in HELD], i32) * (1 - 2 * core)
    whose = jnp.array([w for _, w in HELD], i32)
    spots = (2 * x + yhi * 4 + ylo + 3 * z + offset + 16) % 8 * 2 + (whose + core) % 2
    owner = lax.dynamic_index_in_dim(block_owner[0], x * 2 + yhi)
    places = jnp.concatenate([spots, owner, z[None]])

    def whole(shape, dtype=bf16):
        return jax.ShapeDtypeStruct(shape, dtype)

    (pair,) = call(
        prepare_kernel,
        [whole((8, 2, 16, A))],
        (targets, entry_mask),
        block_owner,
        block_mask,
    )
    mine = spread(embeddings, ALL, 32, CLASSES).reshape(64, -1)
    mine, pair, places = lax.optimization_barrier((mine, pair, places))
    fourth = send(mine, from_chip(0, 1, 1))
    (both,) = call(join_kernel, [whole((128, mine.shape[1]))], (mine, send(mine, CORES)))
    fetched = [send(both, from_chip(*d)) for d in ((1, 0, 0), (0, 1, 0), (0, 0, 1))]
    direct = [both] + fetched
    first, second = head_in[0], head_out[0]
    width = first.shape[0]
    first_held, bias_held, second_held = hbm(first, bias_in, second)
    activations = [KEPT((512, A), bf16), KEPT((512, A), f32)]
    hidden_d, slopes_d = call(direct_kernel, activations, (first_held, bias_held, *direct))

    pair, both = lax.optimization_barrier((pair, both))
    pair = exchange(pair, ("x", "yhi"))
    passed, pair, hidden_d = lax.optimization_barrier((fetched[0], pair, hidden_d))
    late = [send(piece, CORES) for piece in [passed] + fetched[1:]]
    late += [fourth, send(fourth, CORES)]
    hidden_s, slopes_s, shares = call(
        late_kernel,
        activations + [KEPT((8, A, A), bf16)],
        (*hbm(hidden_d), first, bias_in, second, *late),
        places,
        scratch=[pltpu.VMEM((8, 16, 8, A), f32)],
    )
    sums = exchange(shares, "z")
    (copies,) = call(
        residual_kernel, [whole((8, A, A))], (sums, pair, *hbm(bias_out[None])), places
    )
    back = exchange(copies, "z")
    bias_in_grad, head_out_grad, head_in_grad = call(
        last_kernel,
        [whole((1, A), f32), whole((A, A), f32), whole((width, A), f32)],
        (back, *hbm(hidden_d, hidden_s, slopes_d, slopes_s, second)),
        places,
        fetched=direct + late,
        scratch=[
            pltpu.VMEM((8, 16, 8, A), f32),
            pltpu.VMEM((1024, A), f32),
            pltpu.VMEM((1024, A), bf16),
            pltpu.VMEM((2, 1024, 1024), bf16),
            pltpu.SemaphoreType.DMA((2, 9)),
        ],
        limit=20,
    )
    return head_in_grad[None], bias_in_grad, head_out_grad[None]


def solution(mesh):
    mesh = Mesh(mesh.devices.reshape(4, 2, 4, 2, 8), ALL)
    in_specs = (
        P(ALL, None),
        P(TASK, None, FSDP),
        P(TASK, FSDP),
        P(TASK, FSDP, None),
        P(TASK),
        P(TASK, None),
        P(FSDP, TASK),
        P(FSDP, TASK),
        P(FSDP, TASK),
    )
    out_specs = (P(TASK, None, FSDP), P(TASK, FSDP), P(TASK, FSDP, None))
    return jax.shard_map(local, mesh=mesh, in_specs=in_specs, out_specs=out_specs, check_vma=False)
```

```python
import math

import jax
import jax.numpy as jnp
from jax import lax
from jax.experimental import pallas as pl
from jax.experimental.pallas import tpu as pltpu
from jax.sharding import Mesh
from jax.sharding import PartitionSpec as P

H = 1024
A = 128
KEPT = pltpu.HBM
TASK, FSDP = ("ylo", "core"), ("x", "yhi", "z")
ALL = TASK + FSDP

inv_root_two = 0.7071067811865476
inv_root_two_pi = 0.3989422804014327


def gelu_parts(values):
    normal_cdf = 0.5 * (1.0 + lax.erf(values * inv_root_two))
    density = jnp.exp(-0.5 * values * values) * inv_root_two_pi
    return (values * normal_cdf, normal_cdf + values * density)


def place(i):
    t, f = divmod(i, 64)
    ylo, core = divmod(t, 2)
    x, rest = divmod(f, 16)
    yhi, z = divmod(rest, 8)
    return x, yhi * 4 + ylo, z, core


def flat(x, y, z, core):
    x, y, z = x % 4, y % 8, z % 8
    return (y % 4 * 2 + core) * 64 + x * 16 + y // 4 * 8 + z


def classes():
    groups = {}
    for i in range(512):
        x, y, z, core = place(i)
        groups.setdefault(((2 * x + y + 3 * z) % 8, core), []).append(i)
    return [sorted(groups[k], key=place) for k in sorted(groups)]


def from_chip(dx, dy, dz):
    pairs = []
    for i in range(512):
        x, y, z, core = place(i)
        s = 1 - 2 * core
        pairs.append((flat(x + s * dx, y + s * dy, z + s * dz, core), i))
    return pairs


CLASSES = classes()
CORES = [(i, i ^ 64) for i in range(512)]
HELD = [(0, 0), (0, 1), (2, 0), (2, 1), (1, 0), (1, 1), (3, 0), (3, 1)]
HELD += [(-2, 1), (-2, 0), (-1, 1), (-1, 0), (-3, 1), (-3, 0), (4, 0), (4, 1)]


def exchange(blocks, axis, groups=None):
    return lax.all_to_all(blocks, axis, 0, 0, tiled=True, axis_index_groups=groups)


def spread(block, axis, count, groups=None):
    return exchange(jnp.broadcast_to(block[None], (count,) + block.shape), axis, groups)


def send(block, pairs):
    return lax.ppermute(block, ALL, pairs)


def join_kernel(mine, theirs, both, kept):
    both[:64] = mine[...]
    both[64:] = theirs[...]
    kept[...] = mine[...]


def prepare_kernel(block_owner, block_mask, targets, entry_mask, out):
    row = lax.broadcasted_iota(jnp.int32, (16, A), 0)
    for b in range(8):
        o = block_owner[0, b]
        lanes = pl.ds(pl.multiple_of(o * A, A), A)
        measured = entry_mask[:, lanes] * jnp.where(row < 8, block_mask[0, o], block_mask[1, o])
        out[b, 0] = targets[:, lanes]
        out[b, 1] = measured.astype(jnp.float32).astype(jnp.bfloat16)


def residual_kernel(places, sums, pair, bias_out, out):
    owner, z = places[16], places[17]
    lanes = pl.ds(pl.multiple_of(owner * A, A), A)
    r = lax.broadcasted_iota(jnp.int32, (A, A), 0)
    q = lax.broadcasted_iota(jnp.int32, (A, A), 1)
    row_ylo = (r >> 1) & 3
    row_z = (3 * ((r >> 4) + 32 - 2 * (z >> 1) - 4 * (z & 1) - row_ylo)) & 7
    source = row_ylo * 32 + ((r >> 3) & 1) * 16 + row_z * 2 + (r & 1)
    order = jnp.where(q == source, 1.0, 0.0).astype(jnp.bfloat16)
    target = jnp.dot(
        order, pair[:, 0].reshape(A, A), preferred_element_type=jnp.float32
    )
    measured = jnp.dot(
        order, pair[:, 1].reshape(A, A), preferred_element_type=jnp.float32
    )
    total = sums[0].astype(jnp.float32)
    for j in range(1, 8):
        total = total + sums[j].astype(jnp.float32)
    logits = total + bias_out[:, lanes]
    residual = (measured * (logits - target) * (1.0 / math.sqrt(1024))).astype(jnp.bfloat16)
    for j in range(8):
        out[j] = residual


def forward_kernel(pieces, head_in, bias_in, hidden, slopes):
    start = 0
    for piece in pieces:
        span = slice(start, start + piece.shape[0])
        start += piece.shape[0]
        pre = jnp.dot(piece[...], head_in[...], preferred_element_type=jnp.float32) + bias_in[...]
        activated, slope = gelu_parts(pre)
        hidden[span] = activated.astype(jnp.bfloat16)
        slopes[span] = slope


def direct_kernel(head_in, bias_in, *refs):
    forward_kernel(refs[:-2], head_in, bias_in, *refs[-2:])


def late_kernel(spots, hidden_d, head_in, bias_in, head_out, *refs):
    *pieces, hidden_s, slopes_s, out, wide = refs
    forward_kernel(pieces, head_in, bias_in, hidden_s, slopes_s)
    for part, start in ((hidden_d, 0), (hidden_s, 8)):
        share = jnp.dot(part[...], head_out[...], preferred_element_type=jnp.float32)
        for j in range(8):
            wide[:, spots[start + j]] = share[64 * j : 64 * j + 64].reshape(8, 8, A)
    for z in range(8):
        out[z] = wide[z].reshape(A, A).astype(jnp.bfloat16)


def backward_kernel(
    spots, back, hidden_d, hidden_s, slopes_d, slopes_s, head_out, grad, bias, out, wide, rows
):
    for z in range(8):
        wide[z] = back[z].astype(jnp.float32).reshape(16, 8, A)
    for j in range(16):
        rows[64 * j : 64 * j + 64] = wide[:, spots[j]].reshape(64, A)
    bias_sum = jnp.zeros((1, A), jnp.float32)
    out_sum = jnp.zeros((A, A), jnp.float32)
    start = 0
    for hidden, slopes in ((hidden_d, slopes_d), (hidden_s, slopes_s)):
        span = slice(start, start + hidden.shape[0])
        start += hidden.shape[0]
        res = rows[span].astype(jnp.bfloat16)
        held = lax.dot_general(
            res, head_out[...], (((1,), (1,)), ((), ())), preferred_element_type=jnp.float32
        )
        rounded = (held * slopes[...]).astype(jnp.bfloat16)
        grad[span] = rounded
        bias_sum += jnp.sum(rounded.astype(jnp.float32), axis=0, keepdims=True)
        out_sum += lax.dot_general(
            hidden[...], res, (((0,), (0,)), ((), ())), preferred_element_type=jnp.float32
        )
    bias[...] = bias_sum
    out[...] = out_sum


def last_kernel(spots, back, hidden_d, hidden_s, slopes_d, slopes_s, head_out, *refs):
    *pieces, bias, head_out_grad, out, wide, rows, grad, held, sems = refs
    width = held.shape[2]

    def copies(step):
        slot, start, made = step % 2, 0, []
        for j, piece in enumerate(pieces):
            count = piece.shape[0]
            source = piece.at[:, pl.ds(step * width, width)]
            target = held.at[slot, pl.ds(start, count)]
            made.append(pltpu.make_async_copy(source, target, sems.at[slot, j]))
            start += count
        return made

    steps = out.shape[0] // width
    for step in range(2):
        for copy in copies(step):
            copy.start()
    backward_kernel(
        spots, back, hidden_d, hidden_s, slopes_d, slopes_s, head_out, grad, bias, head_out_grad,
        wide, rows,
    )
    weights = grad[...]
    for step in range(steps):
        for copy in copies(step):
            copy.wait()
        product = lax.dot_general(
            weights, held[step % 2], (((0,), (0,)), ((), ())), preferred_element_type=jnp.float32
        )
        out[step * width : step * width + width] = product.T
        if step + 2 < steps:
            for copy in copies(step + 2):
                copy.start()


def hbm(*arrays):
    return [pltpu.with_memory_space_constraint(array, pltpu.HBM) for array in arrays]


def call(kernel, outs, operands, *scalars, fetched=(), scratch=(), limit=12):
    vmem, anywhere = pl.BlockSpec(memory_space=pltpu.VMEM), pl.BlockSpec(memory_space=pl.ANY)
    smem = pl.BlockSpec(memory_space=pltpu.SMEM)
    return pl.pallas_call(
        kernel,
        out_shape=outs,
        in_specs=[smem] * len(scalars) + [vmem] * len(operands) + [anywhere] * len(fetched),
        out_specs=[vmem] * len(outs),
        scratch_shapes=list(scratch),
        compiler_params=pltpu.CompilerParams(vmem_limit_bytes=limit * 1024 * 1024),
    )(*scalars, *operands, *fetched)


def local(
    embeddings, head_in, bias_in, head_out, bias_out, block_owner, targets, entry_mask, block_mask
):
    ylo, core, x, yhi, z = [lax.axis_index(name) for name in ALL]
    bf16, f32, i32 = jnp.bfloat16, jnp.float32, jnp.int32

    offset = jnp.array([d for d, _ in HELD], i32) * (1 - 2 * core)
    whose = jnp.array([w for _, w in HELD], i32)
    spots = (2 * x + yhi * 4 + ylo + 3 * z + offset + 16) % 8 * 2 + (whose + core) % 2
    owner = lax.dynamic_index_in_dim(block_owner[0], x * 2 + yhi)
    places = jnp.concatenate([spots, owner, z[None]])

    def whole(shape, dtype=bf16):
        return jax.ShapeDtypeStruct(shape, dtype)

    (pair,) = call(
        prepare_kernel,
        [whole((8, 2, 16, A))],
        (targets, entry_mask),
        block_owner,
        block_mask,
    )
    mine = spread(embeddings, ALL, 32, CLASSES).reshape(64, -1)
    mine, pair, places = lax.optimization_barrier((mine, pair, places))
    both, kept = call(
        join_kernel,
        [whole((128, mine.shape[1])), KEPT(mine.shape, bf16)],
        (mine, send(mine, CORES)),
    )
    fourth = send(kept, from_chip(0, 1, 1))
    fetched = [send(both, from_chip(*d)) for d in ((1, 0, 0), (0, 1, 0), (0, 0, 1))]
    direct = [both] + fetched
    first, second = head_in[0], head_out[0]
    width = first.shape[0]
    first_held, bias_held, second_held = hbm(first, bias_in, second)
    activations = [KEPT((512, A), bf16), KEPT((512, A), f32)]
    hidden_d, slopes_d = call(direct_kernel, activations, (first_held, bias_held, *direct))

    pair, both = lax.optimization_barrier((pair, both))
    pair = exchange(pair, ("x", "yhi"))
    passed, pair, hidden_d = lax.optimization_barrier((fetched[0], pair, hidden_d))
    late = [send(piece, CORES) for piece in [passed] + fetched[1:]]
    late += [fourth, send(fourth, CORES)]
    hidden_s, slopes_s, shares = call(
        late_kernel,
        activations + [KEPT((8, A, A), bf16)],
        (*hbm(hidden_d), first_held, bias_held, second_held, *late),
        places,
        scratch=[pltpu.VMEM((8, 16, 8, A), f32)],
    )
    sums = exchange(shares, "z")
    (copies,) = call(
        residual_kernel, [whole((8, A, A))], (sums, pair, *hbm(bias_out[None])), places
    )
    back = exchange(copies, "z")
    bias_in_grad, head_out_grad, head_in_grad = call(
        last_kernel,
        [whole((1, A), f32), whole((A, A), f32), whole((width, A), f32)],
        (back, *hbm(hidden_d, hidden_s, slopes_d, slopes_s, second)),
        places,
        fetched=direct + late,
        scratch=[
            pltpu.VMEM((8, 16, 8, A), f32),
            pltpu.VMEM((1024, A), f32),
            pltpu.VMEM((1024, A), bf16),
            pltpu.VMEM((2, 1024, 1024), bf16),
            pltpu.SemaphoreType.DMA((2, 9)),
        ],
        limit=20,
    )
    return head_in_grad[None], bias_in_grad, head_out_grad[None]


def solution(mesh):
    mesh = Mesh(mesh.devices.reshape(4, 2, 4, 2, 8), ALL)
    in_specs = (
        P(ALL, None),
        P(TASK, None, FSDP),
        P(TASK, FSDP),
        P(TASK, FSDP, None),
        P(TASK),
        P(TASK, None),
        P(FSDP, TASK),
        P(FSDP, TASK),
        P(FSDP, TASK),
    )
    out_specs = (P(TASK, None, FSDP), P(TASK, FSDP), P(TASK, FSDP, None))
    return jax.shard_map(local, mesh=mesh, in_specs=in_specs, out_specs=out_specs, check_vma=False)
```
